32 devices in a mesh: fsdp: 8 (over z, y), grp: 4 (over x, core).
Axes of the slice: x: 2, y: 2, z: 4, core: 2. Of those that a mesh axis runs over, the one named last changes fastest.
Arguments:
- latents: bfloat16 [2048, 512], P('fsdp'), may hold values from -6 to 6
- queries: bfloat16 [2048, 128, 128], P('fsdp', 'grp')
- grad_out: bfloat16 [2048, 128, 128], P('fsdp', 'grp'), may hold values from -6 to 6
- kv_weight: bfloat16 [4, 32, 512, 256], P('grp', 'fsdp'), may hold values from -0.25 to 0.25
- doc_ids: int32 [2048], replicated, may hold values from 0 to 3, never falling along the last dimension, each value on 1 to 1024 neighbouring positions
- block_lists: int32 [32, 4], replicated, may hold values from 0 to 31, as said below
Outputs:
- grad_queries: bfloat16 [2048, 128, 128], P('fsdp', 'grp')
- grad_latents: float32 [2048, 512], P('fsdp', 'grp')
- grad_weight: float32 [4, 32, 512, 256], P('grp', 'fsdp')
The draws below stay inside these ranges and needn't reach their ends.
Inputs may be any that keep to these rules, and one draw needn't show every extreme that they name: `block_lists`: row b belongs to query block b; its first entry is b and its 4 entries differ. Take the 4 rows of one run f (rows f * 4 to f * 4 + 3) without their first entries: for every d from 1 to 6 with f - d >= 0, exactly 2 of these entries, counted with repeats, are blocks of run f - d; all other entries are blocks of run f itself.
All inputs are finite; a program needn't handle non-finite values.
Results may differ from the reference program's by a relative error of at most 0.035.
The reference program's roundings to bfloat16 on the way count: a program that leaves them out, or rounds other values in their place, can miss the bound.
Values may be sent and summed in bfloat16 or wider, within the bound.
A program may use at most 128 MiB of HBM per device.

```python
import math
import jax
import jax.numpy as jnp
import numpy as np
from jax import lax

D_LAT = 512
HEADS = 128
DK = 128
BLK = 64
TOPK = 4
TOK_DEV = 256
TOKENS = 2048
QB = 4
CAP = 2
NBLOCKS = 32
HPG = 32
GROUPS = 4
DOCMAX = 1024
DOCS = 4
N_FSDP = 8


def draw_queries(key, part):
    key_values = jax.random.fold_in(key, 0)
    drawn = jax.random.normal(key_values, (TOKENS, HEADS, DK), jnp.float32)
    return drawn.astype(jnp.bfloat16)


def draw_block_lists(key, part):
    device_count = TOKENS // TOK_DEV
    slot_total = QB * (TOPK - 1)
    key_order, key_base = jax.random.split(key)
    order_scores = jax.random.randint(key_order, (device_count, slot_total), 0, 1 << 16) * slot_total + jnp.arange(slot_total)[None, :]
    sort_order = jnp.argsort(order_scores, axis=1)
    slot_rank = jnp.argsort(sort_order, axis=1)
    distance = 1 + slot_rank // CAP
    device_ids = jnp.arange(device_count)[:, None, None]
    owner_ids = device_ids - distance.reshape(device_count, QB, TOPK - 1)
    base_offset = jax.random.randint(key_base, (device_count, QB, 1), 0, QB)
    column_ids = jnp.arange(1, TOPK)[None, None, :]
    query_ids = jnp.arange(QB)[None, :, None]
    local_far = (base_offset + column_ids) % QB
    local_own = (query_ids + 1 + (base_offset + column_ids) % (QB - 1)) % QB
    chosen = jnp.where(owner_ids < 0, device_ids * QB + local_own, owner_ids * QB + local_far)
    own_column = device_ids * QB + query_ids
    return jnp.concatenate([own_column, chosen], axis=2).reshape(NBLOCKS, TOPK).astype(jnp.int32)


def shard_levels(stream_key, shape, shards, smallest, top_value):
    factor_of = 1.0
    for dim, shards_of in shards:
        steps = jax.random.uniform(jax.random.fold_in(jax.random.fold_in(stream_key, 6), dim), (shards_of,), jnp.float32, smallest / len(shards), top_value / len(shards))
        factor_of = factor_of * jnp.repeat(jnp.exp(steps), shape[dim] // shards_of).reshape((-1,) + (1,) * (len(shape) - 1 - dim))
    return factor_of


def length_profile(number_of, total, bound, slope):
    portions = [(1 << 20) // math.isqrt(grade ** slope) + 1 for grade in range(2, number_of + 1)]
    rest, given = total - bound - (number_of - 1), [1] * (number_of - 1)
    while rest > 0:
        movable = [i for i in range(number_of - 1) if given[i] < bound]
        whole, budget = sum([portions[i] for i in movable]), rest
        for i in movable:
            addition = min(bound - given[i], max(1, budget * portions[i] // whole), rest)
            given[i] = given[i] + addition
            rest = rest - addition
    return np.array([bound] + given)


def ragged_sizes(rng, count, total, bound, slope):
    if count == 2:
        one = jax.random.randint(rng, (), max(1, total - bound), min(bound, total - 1) + 1)
        return jnp.stack([one, total - one])
    lengths = jnp.asarray(length_profile(count, total, bound, slope), jnp.int32)
    twos = (count - 1) // 2
    source_of, receiver = lengths[1:1 + 2 * twos:2], lengths[2:2 + 2 * twos:2]
    room = jnp.minimum(source_of - 1, bound - receiver)
    moved = jax.random.randint(jax.random.fold_in(rng, 1), (twos,), 0, 1 << 20) % (room + 1)
    lengths = lengths.at[1:1 + 2 * twos:2].set(source_of - moved).at[2:2 + 2 * twos:2].set(receiver + moved)
    return lengths[jax.random.permutation(jax.random.fold_in(rng, 2), count)]


def gaussian(own_key, dims, scale, bound, pieces=(), kind=jnp.bfloat16):
    loudness = shard_levels(own_key, dims, pieces, -0.22, 0.18) if pieces else 1.0
    values = jax.random.normal(own_key, dims, jnp.float32) * scale * loudness
    return jnp.minimum(jnp.maximum(values, -bound), bound).astype(kind)


def setup_inputs(seed: int = 0) -> dict:
    streams_of = jax.random.split(jax.random.key(seed), 7)
    latents = gaussian(streams_of[0], (TOKENS, D_LAT), 1.0, 6.0, ((0, 8),))
    queries = draw_queries(jax.random.fold_in(streams_of[6], 71), 0)
    grad_out = gaussian(streams_of[2], (TOKENS, HEADS, DK), 1.0, 6.0, ((0, 8), (1, 4)))
    kv_weight = gaussian(streams_of[3], (GROUPS, HPG, D_LAT, 2 * DK), D_LAT ** -0.5, 0.25, ((0, 4), (1, 8)))
    doc_ids = jnp.searchsorted(jnp.cumsum(ragged_sizes(streams_of[4], DOCS, TOKENS, DOCMAX, 2)), jnp.arange(TOKENS), side="right").astype(jnp.int32)
    block_lists = draw_block_lists(jax.random.fold_in(streams_of[6], 71), 0)
    return dict(latents=latents, queries=queries, grad_out=grad_out, kv_weight=kv_weight, doc_ids=doc_ids, block_lists=block_lists)


NEG_FILL = -1e30


def reference(latents, queries, grad_out, kv_weight, doc_ids, block_lists):
    head_weights = kv_weight.reshape(HEADS, D_LAT, 2 * DK)
    offsets = jnp.arange(BLK, dtype=jnp.int32)
    key_pos = (block_lists.astype(jnp.int32)[:, :, None] * BLK + offsets[None, None, :]).reshape(NBLOCKS, TOPK * BLK).astype(jnp.int32)
    query_pos = jnp.arange(TOKENS, dtype=jnp.int32).reshape(NBLOCKS, BLK)
    key_doc = jnp.take(doc_ids, key_pos)
    query_doc = jnp.take(doc_ids, query_pos)
    visible = (key_doc[:, None, :] == query_doc[:, :, None]) & (key_pos[:, None, :] <= query_pos[:, :, None])
    flat_pos = key_pos.reshape(-1)
    score_scale = DK ** -0.5
    run_rows = NBLOCKS * TOPK * BLK // N_FSDP
    slot_lat = jnp.take(latents, flat_pos, axis=0).astype(jnp.float32).reshape(N_FSDP, run_rows, D_LAT)

    def one_head(lat_accum, head_inputs):
        w_head, q_head, g_head = head_inputs
        expanded = jnp.dot(latents, w_head, preferred_element_type=jnp.float32).astype(jnp.bfloat16)
        slot_kv = jnp.take(expanded, flat_pos, axis=0).astype(jnp.float32).reshape(NBLOCKS, TOPK * BLK, 2 * DK)
        key_rows = slot_kv[:, :, :DK]
        value_rows = slot_kv[:, :, DK:]
        q_rows = q_head.astype(jnp.float32).reshape(NBLOCKS, BLK, DK)
        g_rows = g_head.astype(jnp.float32).reshape(NBLOCKS, BLK, DK)
        scores = jnp.einsum("qbd,qkd->qbk", q_rows, key_rows) * score_scale
        scores = jnp.where(visible, scores, NEG_FILL)
        row_max = jnp.max(scores, axis=-1, keepdims=True)
        exp_scores = jnp.exp(scores - row_max)
        softmax_p = exp_scores / jnp.sum(exp_scores, axis=-1, keepdims=True)
        probs_low = lax.optimization_barrier(softmax_p.astype(jnp.bfloat16)).astype(jnp.float32)
        attended = jnp.einsum("qbk,qkd->qbd", probs_low, value_rows)
        delta_rows = jnp.sum(g_rows * attended, axis=-1, keepdims=True)
        grad_probs = jnp.einsum("qbd,qkd->qbk", g_rows, value_rows)
        grad_scores = lax.optimization_barrier((softmax_p * (grad_probs - delta_rows)).astype(jnp.bfloat16)).astype(jnp.float32)
        grad_q = (jnp.einsum("qbk,qkd->qbd", grad_scores, key_rows) * score_scale).astype(jnp.bfloat16)
        grad_k = (jnp.einsum("qbk,qbd->qkd", grad_scores, q_rows) * score_scale).astype(jnp.bfloat16)
        grad_v = jnp.einsum("qbk,qbd->qkd", probs_low, g_rows).astype(jnp.bfloat16)
        grad_kv = lax.optimization_barrier(jnp.concatenate([grad_k, grad_v], axis=-1).reshape(-1, 2 * DK)).astype(jnp.float32)
        token_kv = jnp.zeros((TOKENS, 2 * DK), jnp.float32).at[flat_pos].add(grad_kv)
        lat_accum = lat_accum + lax.dot_general(token_kv, w_head.astype(jnp.float32), (((1,), (1,)), ((), ())), precision=lax.Precision.HIGHEST)
        partial_w = jnp.einsum("grd,grk->gdk", slot_lat, grad_kv.reshape(N_FSDP, run_rows, 2 * DK), precision=lax.Precision.HIGHEST)
        partial_w = lax.optimization_barrier(partial_w.astype(jnp.bfloat16)).astype(jnp.float32)
        return lat_accum, (grad_q.reshape(TOKENS, DK), jnp.sum(partial_w, axis=0))

    lat_start = jnp.zeros((TOKENS, D_LAT), jnp.float32)
    head_inputs = (head_weights, jnp.transpose(queries, (1, 0, 2)), jnp.transpose(grad_out, (1, 0, 2)))
    grad_latents, stacked = lax.scan(one_head, lat_start, head_inputs)
    grad_heads, grad_w_heads = stacked
    grad_queries = jnp.transpose(grad_heads, (1, 0, 2))
    grad_weight = grad_w_heads.reshape(GROUPS, HPG, D_LAT, 2 * DK)
    return (grad_queries, grad_latents, grad_weight)
```

```python
import functools

import jax
import jax.numpy as jnp
from jax import lax
from jax.experimental import pallas as pl
from jax.experimental.pallas import tpu as pltpu
from jax.sharding import PartitionSpec as P

BLK = 64
TOPK = 4
DOCS = 4
NEG_FILL = -1e30


def attention_kernel(
    lists_ref, kp_ref, lo_ref, q_ref, g_ref, kv_ref, gq_ref, tok_ref, acc_ref, *, scale
):
    run = pl.program_id(0)
    heads, rows, dk = q_ref.shape
    blocks = rows // BLK

    @pl.when(run == 0)
    def _():
        acc_ref[...] = jnp.zeros_like(acc_ref)

    for b in range(blocks):
        here = slice(b * BLK, (b + 1) * BLK)
        block = run * blocks + b
        idx = [lists_ref[block * TOPK + s] for s in range(TOPK)]
        key_pos = kp_ref[b : b + 1, :]
        pos = block * BLK + lax.broadcasted_iota(jnp.int32, (BLK, TOPK * BLK), 0)
        visible = (key_pos <= pos) & (key_pos >= lo_ref[here, :])
        for h in range(heads):
            q = q_ref[h, here, :]
            g = g_ref[h, here, :]
            zero = jnp.zeros_like(q)
            qg = jnp.concatenate(
                [jnp.concatenate([q, zero], axis=1), jnp.concatenate([zero, g], axis=1)], axis=0
            )
            kv = jnp.concatenate([kv_ref[h, i] for i in idx], axis=0)
            both = lax.dot_general(
                qg, kv, (((1,), (1,)), ((), ())), preferred_element_type=jnp.float32
            )
            scores = jnp.where(visible, both[:BLK] * scale, NEG_FILL)
            top = jnp.max(scores, axis=-1, keepdims=True)
            e = jnp.exp(scores - top)
            probs = e / jnp.sum(e, axis=-1, keepdims=True)
            low = probs.astype(jnp.bfloat16)
            grad_probs = both[BLK:]
            delta = jnp.sum(low.astype(jnp.float32) * grad_probs, axis=-1, keepdims=True)
            ds = (probs * (grad_probs - delta)).astype(jnp.bfloat16)
            gq = jnp.dot(ds, kv[:, :dk], preferred_element_type=jnp.float32)
            gq_ref[h, here, :] = (gq * scale).astype(jnp.bfloat16)
            sides = jnp.concatenate([ds, low], axis=0)
            dkv = lax.dot_general(
                sides, qg, (((0,), (0,)), ((), ())), preferred_element_type=jnp.float32
            )
            for s in range(TOPK):
                acc_ref[h, idx[s]] += dkv[s * BLK : (s + 1) * BLK]

    @pl.when(run == pl.num_programs(0) - 1)
    def _():
        for h in range(heads):
            part = acc_ref[h]
            tok_ref[h, :, :, :dk] = (part[:, :, :dk] * scale).astype(jnp.bfloat16)
            tok_ref[h, :, :, dk:] = part[:, :, dk:].astype(jnp.bfloat16)


def attention(lists, key_pos, lo, q, g, kv):
    runs, heads, rows, dk = q.shape
    nb = kv.shape[1]
    blocks = rows // BLK
    whole = pl.BlockSpec(
        kv.shape, lambda r, lists: (0, 0, 0, 0), pipeline_mode=pl.Buffered(1)
    )
    act = pl.BlockSpec((None, heads, rows, dk), lambda r, lists: (r, 0, 0, 0))
    pairs = nb * heads
    return pl.pallas_call(
        functools.partial(attention_kernel, scale=dk**-0.5),
        grid_spec=pltpu.PrefetchScalarGridSpec(
            num_scalar_prefetch=1,
            grid=(runs,),
            in_specs=[
                pl.BlockSpec((None, blocks, TOPK * BLK), lambda r, lists: (r, 0, 0)),
                pl.BlockSpec((rows, 1), lambda r, lists: (r, 0)),
                act,
                act,
                whole,
            ],
            out_specs=[act, whole],
            scratch_shapes=[pltpu.VMEM(kv.shape, jnp.float32)],
        ),
        out_shape=[
            jax.ShapeDtypeStruct(q.shape, jnp.bfloat16),
            jax.ShapeDtypeStruct(kv.shape, jnp.bfloat16),
        ],
        compiler_params=pltpu.CompilerParams(
            dimension_semantics=("arbitrary",), vmem_limit_bytes=48 * 1024 * 1024
        ),
        cost_estimate=pl.CostEstimate(
            flops=pairs * 5 * 2 * BLK * TOPK * BLK * dk,
            bytes_accessed=3 * 2 * q.size + 4 * kv.size,
            transcendentals=pairs * BLK * TOPK * BLK,
        ),
    )(lists.reshape(-1), key_pos, lo, q, g, kv)


def per_device(latents, queries, grad_out, kv_weight, doc_ids, block_lists):
    n = lax.axis_size("fsdp")
    rows, lat_width = latents.shape
    dk = queries.shape[2]
    heads = kv_weight.shape[1]
    tokens = doc_ids.shape[0]
    nb = tokens // BLK
    w = kv_weight[0]

    all_lat = lax.all_gather(latents, "fsdp", axis=0, tiled=True)

    def by_owner(x):
        return x.reshape(rows, n, heads, dk).transpose(1, 2, 0, 3)

    q = lax.all_to_all(by_owner(queries), "fsdp", 0, 0, tiled=True)
    g = lax.all_to_all(by_owner(grad_out), "fsdp", 0, 0, tiled=True)

    starts = [jnp.sum((doc_ids < v).astype(jnp.int32)) for v in range(DOCS)]
    lo = sum(jnp.where(doc_ids == v, starts[v], 0) for v in range(DOCS))
    key_pos = (block_lists[:, :, None] * BLK + jnp.arange(BLK, dtype=jnp.int32)).reshape(
        n, nb // n, TOPK * BLK
    )

    kv = jnp.einsum("tl,hlk->htk", all_lat, w, preferred_element_type=jnp.float32)
    kv = kv.astype(jnp.bfloat16).reshape(heads, nb, BLK, 2 * dk)
    gq, tok = attention(block_lists, key_pos, lo[:, None], q, g, kv)
    tok = tok.reshape(heads, tokens, 2 * dk)

    lat_part = jnp.einsum("htk,hlk->tl", tok, w, preferred_element_type=jnp.float32)
    shares = lax.psum_scatter(
        lat_part.astype(jnp.bfloat16), "grp", scatter_dimension=1, tiled=True
    )
    grad_latents = lax.psum_scatter(
        shares.astype(jnp.float32), "fsdp", scatter_dimension=0, tiled=True
    )
    back = lax.all_to_all(gq, "fsdp", 0, 0, tiled=True)
    grad_queries = back.transpose(2, 0, 1, 3).reshape(rows, n * heads, dk)
    grad_weight = jnp.einsum("tl,htk->hlk", all_lat, tok, preferred_element_type=jnp.float32)
    return (grad_queries, grad_latents, grad_weight[None])


def solution(mesh):
    return jax.shard_map(
        per_device,
        mesh=mesh,
        in_specs=(
            P("fsdp", None),
            P("fsdp", "grp", None),
            P("fsdp", "grp", None),
            P("grp", "fsdp", None, None),
            P(),
            P(),
        ),
        out_specs=(P("fsdp", "grp", None), P("fsdp", "grp"), P("grp", "fsdp", None, None)),
        check_vma=False,
    )
```

```python
import functools

import jax
import jax.numpy as jnp
from jax import lax
from jax.experimental import pallas as pl
from jax.experimental.pallas import tpu as pltpu
from jax.sharding import PartitionSpec as P

BLK = 64
TOPK = 4
DOCS = 4
NEG_FILL = -1e30


def attention_kernel(
    lists_ref, kp_ref, lo_ref, qg_ref, kv_ref, gq_ref, tok_ref, acc_ref, *, scale
):
    run = pl.program_id(0)
    _, heads, rows, dk = qg_ref.shape
    blocks = rows // BLK

    @pl.when(run == 0)
    def _():
        acc_ref[...] = jnp.zeros_like(acc_ref)

    for b in range(blocks):
        here = slice(b * BLK, (b + 1) * BLK)
        block = run * blocks + b
        idx = [lists_ref[block * TOPK + s] for s in range(TOPK)]
        key_pos = kp_ref[b : b + 1, :]
        pos = block * BLK + lax.broadcasted_iota(jnp.int32, (BLK, TOPK * BLK), 0)
        visible = (key_pos <= pos) & (key_pos >= lo_ref[here, :])
        for h in range(heads):
            q = qg_ref[0, h, here, :]
            g = qg_ref[1, h, here, :]
            zero = jnp.zeros_like(q)
            qg = jnp.concatenate(
                [jnp.concatenate([q, zero], axis=1), jnp.concatenate([zero, g], axis=1)], axis=0
            )
            kv = jnp.concatenate([kv_ref[h, i] for i in idx], axis=0)
            both = lax.dot_general(
                qg, kv, (((1,), (1,)), ((), ())), preferred_element_type=jnp.float32
            )
            scores = jnp.where(visible, both[:BLK] * scale, NEG_FILL)
            top = jnp.max(scores, axis=-1, keepdims=True)
            e = jnp.exp(scores - top)
            probs = e / jnp.sum(e, axis=-1, keepdims=True)
            low = probs.astype(jnp.bfloat16)
            grad_probs = both[BLK:]
            delta = jnp.sum(low.astype(jnp.float32) * grad_probs, axis=-1, keepdims=True)
            ds = (probs * (grad_probs - delta)).astype(jnp.bfloat16)
            gq = jnp.dot(ds, kv[:, :dk], preferred_element_type=jnp.float32)
            gq_ref[h, here, :] = (gq * scale).astype(jnp.bfloat16)
            sides = jnp.concatenate([ds, low], axis=0)
            dkv = lax.dot_general(
                sides, qg, (((0,), (0,)), ((), ())), preferred_element_type=jnp.float32
            )
            for s in range(TOPK):
                acc_ref[h, idx[s]] += dkv[s * BLK : (s + 1) * BLK]

    @pl.when(run == pl.num_programs(0) - 1)
    def _():
        for h in range(heads):
            part = acc_ref[h]
            tok_ref[h, :, :, :dk] = (part[:, :, :dk] * scale).astype(jnp.bfloat16)
            tok_ref[h, :, :, dk:] = part[:, :, dk:].astype(jnp.bfloat16)


def attention(lists, key_pos, lo, qg, kv):
    runs, _, heads, rows, dk = qg.shape
    nb = kv.shape[1]
    blocks = rows // BLK
    whole = pl.BlockSpec(
        kv.shape, lambda r, lists: (0, 0, 0, 0), pipeline_mode=pl.Buffered(1)
    )
    act = pl.BlockSpec((None, heads, rows, dk), lambda r, lists: (r, 0, 0, 0))
    pairs = nb * heads
    return pl.pallas_call(
        functools.partial(attention_kernel, scale=dk**-0.5),
        grid_spec=pltpu.PrefetchScalarGridSpec(
            num_scalar_prefetch=1,
            grid=(runs,),
            in_specs=[
                pl.BlockSpec((None, blocks, TOPK * BLK), lambda r, lists: (r, 0, 0)),
                pl.BlockSpec((rows, 1), lambda r, lists: (r, 0)),
                pl.BlockSpec((None, 2, heads, rows, dk), lambda r, lists: (r, 0, 0, 0, 0)),
                whole,
            ],
            out_specs=[act, whole],
            scratch_shapes=[pltpu.VMEM(kv.shape, jnp.float32)],
        ),
        out_shape=[
            jax.ShapeDtypeStruct((runs, heads, rows, dk), jnp.bfloat16),
            jax.ShapeDtypeStruct(kv.shape, jnp.bfloat16),
        ],
        compiler_params=pltpu.CompilerParams(
            dimension_semantics=("arbitrary",), vmem_limit_bytes=48 * 1024 * 1024
        ),
        cost_estimate=pl.CostEstimate(
            flops=pairs * 5 * 2 * BLK * TOPK * BLK * dk,
            bytes_accessed=3 * qg.size + 4 * kv.size,
            transcendentals=pairs * BLK * TOPK * BLK,
        ),
    )(lists.reshape(-1), key_pos, lo, qg, kv)


def per_device(latents, queries, grad_out, kv_weight, doc_ids, block_lists):
    n = lax.axis_size("fsdp")
    rows, lat_width = latents.shape
    dk = queries.shape[2]
    heads = kv_weight.shape[1]
    tokens = doc_ids.shape[0]
    nb = tokens // BLK

    all_lat = lax.all_gather(latents, "fsdp", axis=0, tiled=True)

    sizes = [h for h in (heads // 2, heads - heads // 2) if h]
    spans = [slice(sum(sizes[:i]), sum(sizes[: i + 1])) for i in range(len(sizes))]

    def by_owner(x, span):
        return x.reshape(rows, n, heads, dk)[:, :, span].transpose(1, 2, 0, 3)

    arrived = [
        lax.all_to_all(
            jnp.stack([by_owner(queries, span), by_owner(grad_out, span)], axis=1),
            "fsdp",
            0,
            0,
            tiled=True,
        )
        for span in spans
    ]

    starts = [jnp.sum((doc_ids < v).astype(jnp.int32)) for v in range(DOCS)]
    lo = sum(jnp.where(doc_ids == v, starts[v], 0) for v in range(DOCS))
    key_pos = (block_lists[:, :, None] * BLK + jnp.arange(BLK, dtype=jnp.int32)).reshape(
        n, nb // n, TOPK * BLK
    )

    back, grad_w, lat_part = [], [], 0.0
    for span, qg in zip(spans, arrived):
        w = kv_weight[0, span]
        kv = jnp.einsum("tl,hlk->htk", all_lat, w, preferred_element_type=jnp.float32)
        kv = kv.astype(jnp.bfloat16).reshape(-1, nb, BLK, 2 * dk)
        gq, tok = attention(block_lists, key_pos, lo[:, None], qg, kv)
        back.append(lax.all_to_all(gq, "fsdp", 0, 0, tiled=True))
        tok = tok.reshape(-1, tokens, 2 * dk)
        lat_part += jnp.einsum("htk,hlk->tl", tok, w, preferred_element_type=jnp.float32)
        grad_w.append(
            jnp.einsum("tl,htk->hlk", all_lat, tok, preferred_element_type=jnp.float32)
        )

    shares = lax.psum_scatter(
        lat_part.astype(jnp.bfloat16), "grp", scatter_dimension=1, tiled=True
    )
    pieces = lax.all_to_all(shares.reshape(n, rows, -1), "fsdp", 0, 0, tiled=True)
    grad_latents = jnp.sum(pieces.astype(jnp.float32), axis=0)
    grad_queries = jnp.concatenate([x.transpose(2, 0, 1, 3) for x in back], axis=2)
    grad_queries = grad_queries.reshape(rows, n * heads, dk)
    grad_weight = jnp.concatenate(grad_w, axis=0)
    return (grad_queries, grad_latents, grad_weight[None])


def solution(mesh):
    return jax.shard_map(
        per_device,
        mesh=mesh,
        in_specs=(
            P("fsdp", None),
            P("fsdp", "grp", None),
            P("fsdp", "grp", None),
            P("grp", "fsdp", None, None),
            P(),
            P(),
        ),
        out_specs=(P("fsdp", "grp", None), P("fsdp", "grp"), P("grp", "fsdp", None, None)),
        check_vma=False,
    )
```

```python
import functools

import jax
import jax.numpy as jnp
from jax import lax
from jax.experimental import pallas as pl
from jax.experimental.pallas import tpu as pltpu
from jax.sharding import PartitionSpec as P

BLK = 64
TOPK = 4
DOCS = 4
NEG_FILL = -1e30


def attention_kernel(
    lists_ref, kp_ref, lo_ref, qg_ref, kv_ref, gq_ref, tok_ref, acc_ref, *, scale
):
    run = pl.program_id(0)
    _, heads, rows, dk = qg_ref.shape
    blocks = rows // BLK

    @pl.when(run == 0)
    def _():
        acc_ref[...] = jnp.zeros_like(acc_ref)

    for b in range(blocks):
        here = slice(b * BLK, (b + 1) * BLK)
        block = run * blocks + b
        idx = [lists_ref[block * TOPK + s] for s in range(TOPK)]
        key_pos = kp_ref[b : b + 1, :]
        pos = block * BLK + lax.broadcasted_iota(jnp.int32, (BLK, TOPK * BLK), 0)
        visible = (key_pos <= pos) & (key_pos >= lo_ref[here, :])
        for h in range(heads):
            q = qg_ref[0, h, here, :]
            g = qg_ref[1, h, here, :]
            zero = jnp.zeros_like(q)
            qg = jnp.concatenate(
                [jnp.concatenate([q, zero], axis=1), jnp.concatenate([zero, g], axis=1)], axis=0
            )
            kv = jnp.concatenate([kv_ref[h, i] for i in idx], axis=0)
            both = lax.dot_general(
                qg, kv, (((1,), (1,)), ((), ())), preferred_element_type=jnp.float32
            )
            scores = jnp.where(visible, both[:BLK] * scale, NEG_FILL)
            top = jnp.max(scores, axis=-1, keepdims=True)
            e = jnp.exp(scores - top)
            probs = e / jnp.sum(e, axis=-1, keepdims=True)
            low = probs.astype(jnp.bfloat16)
            grad_probs = both[BLK:]
            delta = jnp.sum(low.astype(jnp.float32) * grad_probs, axis=-1, keepdims=True)
            ds = (probs * (grad_probs - delta)).astype(jnp.bfloat16)
            gq = jnp.dot(ds, kv[:, :dk], preferred_element_type=jnp.float32)
            gq_ref[h, here, :] = (gq * scale).astype(jnp.bfloat16)
            sides = jnp.concatenate([ds, low], axis=0)
            dkv = lax.dot_general(
                sides, qg, (((0,), (0,)), ((), ())), preferred_element_type=jnp.float32
            )
            for s in range(TOPK):
                acc_ref[h, idx[s]] += dkv[s * BLK : (s + 1) * BLK]

    @pl.when(run == pl.num_programs(0) - 1)
    def _():
        for h in range(heads):
            part = acc_ref[h]
            tok_ref[h, :, :, :dk] = (part[:, :, :dk] * scale).astype(jnp.bfloat16)
            tok_ref[h, :, :, dk:] = part[:, :, dk:].astype(jnp.bfloat16)


def attention(lists, key_pos, lo, qg, kv):
    runs, _, heads, rows, dk = qg.shape
    nb = kv.shape[1]
    blocks = rows // BLK
    whole = pl.BlockSpec(
        kv.shape, lambda r, lists: (0, 0, 0, 0), pipeline_mode=pl.Buffered(1)
    )
    act = pl.BlockSpec((None, heads, rows, dk), lambda r, lists: (r, 0, 0, 0))
    pairs = nb * heads
    return pl.pallas_call(
        functools.partial(attention_kernel, scale=dk**-0.5),
        grid_spec=pltpu.PrefetchScalarGridSpec(
            num_scalar_prefetch=1,
            grid=(runs,),
            in_specs=[
                pl.BlockSpec((None, blocks, TOPK * BLK), lambda r, lists: (r, 0, 0)),
                pl.BlockSpec((rows, 1), lambda r, lists: (r, 0)),
                pl.BlockSpec((None, 2, heads, rows, dk), lambda r, lists: (r, 0, 0, 0, 0)),
                whole,
            ],
            out_specs=[act, whole],
            scratch_shapes=[pltpu.VMEM(kv.shape, jnp.float32)],
        ),
        out_shape=[
            jax.ShapeDtypeStruct((runs, heads, rows, dk), jnp.bfloat16),
            jax.ShapeDtypeStruct(kv.shape, jnp.bfloat16),
        ],
        compiler_params=pltpu.CompilerParams(
            dimension_semantics=("arbitrary",), vmem_limit_bytes=48 * 1024 * 1024
        ),
        cost_estimate=pl.CostEstimate(
            flops=pairs * 5 * 2 * BLK * TOPK * BLK * dk,
            bytes_accessed=3 * qg.size + 4 * kv.size,
            transcendentals=pairs * BLK * TOPK * BLK,
        ),
    )(lists.reshape(-1), key_pos, lo, qg, kv)


def per_device(latents, queries, grad_out, kv_weight, doc_ids, block_lists):
    n = lax.axis_size("fsdp")
    rows, lat_width = latents.shape
    dk = queries.shape[2]
    heads = kv_weight.shape[1]
    tokens = doc_ids.shape[0]
    nb = tokens // BLK

    all_lat = lax.all_gather(latents, "fsdp", axis=0, tiled=True)

    sizes = [h for h in (heads // 2, heads - heads // 2) if h]
    spans = [slice(sum(sizes[:i]), sum(sizes[: i + 1])) for i in range(len(sizes))]

    def by_owner(x, span):
        return x.reshape(rows, n, heads, dk)[:, :, span].transpose(1, 2, 0, 3)

    arrived = [
        lax.all_to_all(
            jnp.stack([by_owner(queries, span), by_owner(grad_out, span)], axis=1),
            "fsdp",
            0,
            0,
            tiled=True,
        )
        for span in spans
    ]

    starts = [jnp.sum((doc_ids < v).astype(jnp.int32)) for v in range(DOCS)]
    lo = sum(jnp.where(doc_ids == v, starts[v], 0) for v in range(DOCS))
    key_pos = (block_lists[:, :, None] * BLK + jnp.arange(BLK, dtype=jnp.int32)).reshape(
        n, nb // n, TOPK * BLK
    )

    back, grad_w, lat_part = [], [], 0.0
    for span, qg in zip(spans, arrived):
        w = kv_weight[0, span]
        kv = jnp.einsum("tl,hlk->htk", all_lat, w, preferred_element_type=jnp.float32)
        kv = kv.astype(jnp.bfloat16).reshape(-1, nb, BLK, 2 * dk)
        gq, tok = attention(block_lists, key_pos, lo[:, None], qg, kv)
        back.append(lax.all_to_all(gq, "fsdp", 0, 0, tiled=True))
        tok = tok.reshape(-1, tokens, 2 * dk)
        lat_part += jnp.einsum("hlk,htk->lt", w, tok, preferred_element_type=jnp.float32)
        grad_w.append(
            jnp.einsum("tl,htk->hlk", all_lat, tok, preferred_element_type=jnp.float32)
        )

    lat_low, back[0] = lax.optimization_barrier((lat_part.astype(jnp.bfloat16), back[0]))
    shares = lax.psum_scatter(lat_low, "grp", scatter_dimension=0, tiled=True).T
    pieces = lax.all_to_all(shares.reshape(n, rows, -1), "fsdp", 0, 0, tiled=True)
    grad_latents = jnp.sum(pieces.astype(jnp.float32), axis=0)
    grad_queries = jnp.concatenate([x.transpose(2, 0, 1, 3) for x in back], axis=2)
    grad_queries = grad_queries.reshape(rows, n * heads, dk)
    grad_weight = jnp.concatenate(grad_w, axis=0)
    return (grad_queries, grad_latents, grad_weight[None])


def solution(mesh):
    return jax.shard_map(
        per_device,
        mesh=mesh,
        in_specs=(
            P("fsdp", None),
            P("fsdp", "grp", None),
            P("fsdp", "grp", None),
            P("grp", "fsdp", None, None),
            P(),
            P(),
        ),
        out_specs=(P("fsdp", "grp", None), P("fsdp", "grp"), P("grp", "fsdp", None, None)),
        check_vma=False,
    )
```
